256 devices in a mesh: res: 256 (over x, y, z, core).
Axes of the slice: x: 4, y: 4, z: 8, core: 2. Of those that a mesh axis runs over, the one named last changes fastest.
Arguments:
- homolog_features: bfloat16 [256, 6144, 256], P(None, 'res'), may hold values from -6 to 6
- standardize_scale: float32 [256], replicated, may hold values from 0.25 to 1.75
- standardize_shift: float32 [256], replicated, may hold values from -3 to 3
- first_map_matrix: bfloat16 [256, 32], replicated, may hold values from -0.375 to 0.375
- first_map_intercept: float32 [32], replicated, may hold values from -3 to 3
- other_map_matrix: bfloat16 [256, 32], replicated, may hold values from -0.375 to 0.375
- other_map_intercept: float32 [32], replicated, may hold values from -3 to 3
- final_map_matrix: bfloat16 [1024, 128], replicated, may hold values from -0.1875 to 0.1875
- final_map_intercept: float32 [128], replicated, may hold values from -3 to 3
- coverage_lengths: int32 [6144], P('res'), may hold values from 0 to 256
- couple_features: float32 [6144, 216, 128], P('res'), may hold values from -6 to 6
Outputs:
- pair_out: float32 [6144, 216, 128], P('res')
The draws below stay inside these ranges and needn't reach their ends.
All inputs are finite; a program needn't handle non-finite values.
Results may differ from the reference program's by a relative error of at most 0.0035.
Values may be sent and summed in bfloat16 or wider, within the bound.
No kernel may reach another device: no remote copies, remote signals or barrier semaphores. Data moves between devices by JAX's collectives and lax.ppermute only.
A program may use at most 128 MiB of HBM per device.

```python
import jax
import jax.numpy as jnp
from jax import lax

FEATURE_DIM = 256
HIDDEN_WIDTH = 32
C_Z = 128
HOMOLOG_NUMBER = 256
LOCAL_POSITIONS = 24
WIN = 4
CHAIN_LENGTH = 6144
COLS = 216
N_RES = 256


def plant(values, rng, least, high):
    spot = [jax.random.randint(jax.random.fold_in(rng, axis), (), 0, length) for axis, length in enumerate(values.shape)]
    main_axis = values.shape.index(max(values.shape))
    next_to = spot[:main_axis] + [(spot[main_axis] + 1) % values.shape[main_axis]] + spot[main_axis + 1:]
    return values.at[tuple(spot)].set(least).at[tuple(next_to)].set(high)


def level_of(key, dims, cuts, smallest, largest):
    gain = 1.0
    for axis_at, blocks in cuts:
        draws = jax.random.uniform(jax.random.fold_in(jax.random.fold_in(key, 6), axis_at), (blocks,), jnp.float32, smallest / len(cuts), largest / len(cuts))
        gain = gain * jnp.repeat(jnp.exp(draws), dims[axis_at] // blocks).reshape((-1,) + (1,) * (len(dims) - 1 - axis_at))
    return gain


def normal_values(rng, shape, width, reach, split=(), kind=jnp.bfloat16):
    loudness = level_of(rng, shape, split, -0.22, 0.18) if split else 1.0
    array = jax.random.normal(rng, shape, jnp.float32) * width * loudness
    return jnp.minimum(jnp.maximum(array, -reach), reach).astype(kind)


def setup_inputs(seed: int = 0) -> dict:
    splits = jax.random.split(jax.random.key(seed), 12)
    return {
        "homolog_features": normal_values(splits[0], (HOMOLOG_NUMBER, CHAIN_LENGTH, FEATURE_DIM), 1.0, 6.0, ((1, 256),)),
        "standardize_scale": jnp.clip(1.0 + 0.15 * jax.random.normal(splits[1], (FEATURE_DIM,), jnp.float32), 0.25, 1.75),
        "standardize_shift": normal_values(splits[2], (FEATURE_DIM,), 0.5, 3.0, (), jnp.float32),
        "first_map_matrix": normal_values(splits[3], (FEATURE_DIM, HIDDEN_WIDTH), FEATURE_DIM ** -0.5, 0.375),
        "first_map_intercept": normal_values(splits[4], (HIDDEN_WIDTH,), 0.5, 3.0, (), jnp.float32),
        "other_map_matrix": normal_values(splits[5], (FEATURE_DIM, HIDDEN_WIDTH), FEATURE_DIM ** -0.5, 0.375),
        "other_map_intercept": normal_values(splits[6], (HIDDEN_WIDTH,), 0.5, 3.0, (), jnp.float32),
        "final_map_matrix": normal_values(splits[7], (HIDDEN_WIDTH * HIDDEN_WIDTH, C_Z), (HIDDEN_WIDTH * HIDDEN_WIDTH) ** -0.5, 0.1875),
        "final_map_intercept": normal_values(splits[8], (C_Z,), 0.5, 3.0, (), jnp.float32),
        "coverage_lengths": plant(jax.random.randint(splits[9], (CHAIN_LENGTH,), 0, HOMOLOG_NUMBER + 1), jax.random.fold_in(splits[9], 1), 0, HOMOLOG_NUMBER).astype(jnp.int32),
        "couple_features": normal_values(splits[10], (CHAIN_LENGTH, COLS, C_Z), 1.0, 6.0, ((0, 256),), jnp.float32),
    }


def projected_row_values(homolog_lines, depth_row_slices, standardize_scale, standardize_shift, first_map_matrix, first_map_intercept, other_map_matrix, other_map_intercept):
    value_entries = homolog_lines.astype(jnp.float32)
    average = lax.optimization_barrier(jnp.mean(value_entries, axis=-1, keepdims=True))
    centred = value_entries - average
    variance = lax.optimization_barrier(jnp.mean(centred * centred, axis=-1, keepdims=True))
    normed = (centred * lax.rsqrt(variance + 1e-05) * standardize_scale + standardize_shift).astype(jnp.bfloat16)
    seq_index = jnp.arange(value_entries.shape[0], dtype=jnp.int32)
    seq_mask = (seq_index[:, None] < depth_row_slices[None, :]).astype(jnp.float32)[:, :, None]
    left_proj = ((jnp.dot(normed, first_map_matrix, preferred_element_type=jnp.float32) + first_map_intercept) * seq_mask).astype(jnp.bfloat16)
    right_proj = ((jnp.dot(normed, other_map_matrix, preferred_element_type=jnp.float32) + other_map_intercept) * seq_mask).astype(jnp.bfloat16)
    return (left_proj, right_proj)

def form_tile(left_rows, right_cols, depth_row_slices, depth_cols, final_map_matrix, final_map_intercept):
    outer_sum = jnp.einsum('sic,sje->ijce', left_rows.astype(jnp.float32), right_cols.astype(jnp.float32))
    outer_flat = outer_sum.astype(jnp.bfloat16).reshape(left_rows.shape[1] * right_cols.shape[1], -1)
    projected = jnp.dot(outer_flat, final_map_matrix, preferred_element_type=jnp.float32) + final_map_intercept
    pair_count = jnp.maximum(jnp.minimum(depth_row_slices.astype(jnp.float32)[:, None], depth_cols.astype(jnp.float32)[None, :]), 1.0)
    result = projected / pair_count.reshape(-1, 1)
    return result.reshape(left_rows.shape[1], right_cols.shape[1], -1)

def reference(homolog_features, standardize_scale, standardize_shift, first_map_matrix, first_map_intercept, other_map_matrix, other_map_intercept, final_map_matrix, final_map_intercept, coverage_lengths, couple_features):

    def proj_block(block):
        initial_position = (block * LOCAL_POSITIONS).astype(jnp.int32)
        homolog_lines = lax.dynamic_slice_in_dim(homolog_features, initial_position, LOCAL_POSITIONS, 1)
        depth_row_slices = lax.dynamic_slice_in_dim(coverage_lengths, initial_position, LOCAL_POSITIONS, 0)
        return projected_row_values(homolog_lines, depth_row_slices, standardize_scale, standardize_shift, first_map_matrix, first_map_intercept, other_map_matrix, other_map_intercept)
    block_ids = jnp.arange(N_RES, dtype=jnp.int32)
    left_all, right_all = lax.map(proj_block, block_ids)
    depth_all = coverage_lengths.reshape(N_RES, LOCAL_POSITIONS)
    zero_blocks = jnp.zeros((WIN,) + right_all.shape[1:], right_all.dtype)
    right_pad = jnp.concatenate([zero_blocks, right_all, zero_blocks], axis=0)
    zero_depth = jnp.zeros((WIN, LOCAL_POSITIONS), coverage_lengths.dtype)
    depth_pad = jnp.concatenate([zero_depth, depth_all, zero_depth], axis=0)

    def row_block(block):
        left_rows = lax.dynamic_index_in_dim(left_all, block, 0, keepdims=False)
        depth_row_slices = lax.dynamic_index_in_dim(depth_all, block, 0, keepdims=False)
        pieces = []
        for offset in range(2 * WIN + 1):
            right_cols = lax.dynamic_index_in_dim(right_pad, block + offset, 0, keepdims=False)
            depth_cols = lax.dynamic_index_in_dim(depth_pad, block + offset, 0, keepdims=False)
            tile_value = form_tile(left_rows, right_cols, depth_row_slices, depth_cols, final_map_matrix, final_map_intercept)
            column_block = block + (offset - WIN)
            inside = (column_block >= 0) & (column_block < N_RES)
            pieces.append(jnp.where(inside, tile_value, 0.0))
        return jnp.concatenate(pieces, axis=1)
    band = lax.map(row_block, block_ids)
    band = band.reshape(N_RES * LOCAL_POSITIONS, band.shape[2], band.shape[3])
    return couple_features + band
```

```python
import functools

import jax
import jax.numpy as jnp
from jax import lax
from jax.experimental import pallas as pl
from jax.experimental.pallas import tpu as pltpu
from jax.sharding import PartitionSpec as P

WIN = 4
ROWS = 24
WIDTH = 32
SEQS = 256
STEP = 32
FLAT = ROWS * WIDTH
SENT = FLAT + 16

BF16 = jnp.bfloat16
F32 = jnp.float32
NT = (((1,), (1,)), ((), ()))


def as_column(row, count):
    width = row.shape[1]
    wide = jnp.broadcast_to(row, (count, width))
    at = lax.broadcasted_iota(jnp.int32, (count, width), 1)
    down = lax.broadcasted_iota(jnp.int32, (count, width), 0)
    return jnp.sum(jnp.where(at == down, wide, 0.0), axis=1, keepdims=True)


def project_kernel(
    depth_ref,
    lines_ref,
    scale_ref,
    shift_ref,
    first_ref,
    first_bias_ref,
    other_ref,
    other_bias_ref,
    left_ref,
    right_ref,
    low_ref,
    high_ref,
    maps_ref,
    turn_ref,
    right_low_ref,
    right_high_ref,
):
    step = pl.program_id(0)
    scale = scale_ref[...]
    shift = shift_ref[...]
    part = 4
    for c in range(STEP // part):
        x = lines_ref[c * part : (c + 1) * part].astype(F32).reshape(part * ROWS, -1)
        centred = x - jnp.mean(x, axis=1, keepdims=True)
        variance = jnp.mean(centred * centred, axis=1, keepdims=True)
        normed = centred * lax.rsqrt(variance + 1e-05) * scale + shift
        at = pl.ds(pl.multiple_of((step * STEP + c * part) * ROWS, 8), part * ROWS)
        low_ref[at, :] = normed[:, :128]
        high_ref[at, :] = normed[:, 128:]

    @pl.when(step == SEQS // STEP - 1)
    def _():
        maps_ref[:WIDTH, :] = first_ref[...].astype(F32).T
        turned = other_ref[...].astype(F32).T
        first_bias = as_column(first_bias_ref[...], WIDTH)
        other_bias = jnp.broadcast_to(as_column(other_bias_ref[...], WIDTH), (WIDTH, 128))
        turn_ref[0] = turned[:, :128]
        turn_ref[1] = turned[:, 128:]
        turn_ref[2] = other_bias
        biases = [jnp.broadcast_to(first_bias, (WIDTH, 128))]
        for k in range(4):
            for half in range(2):
                maps_ref[WIDTH + 8 * k : WIDTH + 8 * k + 8, half * 128 : half * 128 + 128] = (
                    turn_ref[half, pl.ds(k, 8, stride=4), :]
                )
            biases.append(turn_ref[2, pl.ds(k, 8, stride=4), :])
        bias = jnp.concatenate(biases, axis=0)
        bias = jnp.concatenate([bias, bias], axis=1)
        maps = maps_ref[...].astype(BF16)
        seq = lax.broadcasted_iota(jnp.int32, (2 * WIDTH, SEQS), 1)
        lane = lax.broadcasted_iota(jnp.int32, (16, SEQS), 1)
        depths = jnp.zeros((16, SEQS), F32)
        for i in range(ROWS):
            depth = depth_ref[i]
            rows = jnp.concatenate(
                [low_ref[pl.ds(i, SEQS, stride=ROWS), :], high_ref[pl.ds(i, SEQS, stride=ROWS), :]],
                axis=1,
            ).astype(BF16)
            both = lax.dot_general(maps, rows, NT, preferred_element_type=F32) + bias
            both = jnp.where(seq < depth, both, 0.0)
            left_ref[i * WIDTH : (i + 1) * WIDTH, :] = both[:WIDTH].astype(BF16)
            right_low_ref[pl.ds(i, WIDTH, stride=ROWS), :] = both[WIDTH:, :128]
            right_high_ref[pl.ds(i, WIDTH, stride=ROWS), :] = both[WIDTH:, 128:]
            depths = jnp.where(lane == i, depth.astype(F32), depths)
        right_ref[:FLAT, :128] = right_low_ref[...].astype(BF16)
        right_ref[:FLAT, 128:] = right_high_ref[...].astype(BF16)
        right_ref[FLAT:, :] = depths.astype(BF16)


def whole(shape):
    return pl.BlockSpec(shape, lambda *_: (0,) * len(shape))


def project(lines, depth, scale, shift, first, first_bias, other, other_bias):
    channels = lines.shape[2]
    return pl.pallas_call(
        project_kernel,
        grid=(SEQS // STEP,),
        in_specs=[
            pl.BlockSpec(memory_space=pltpu.SMEM),
            pl.BlockSpec((STEP, ROWS, channels), lambda s: (s, 0, 0)),
            whole((1, channels)),
            whole((1, channels)),
            whole((channels, WIDTH)),
            whole((1, WIDTH)),
            whole((channels, WIDTH)),
            whole((1, WIDTH)),
        ],
        out_specs=[whole((FLAT, SEQS)), whole((SENT, SEQS))],
        out_shape=[
            jax.ShapeDtypeStruct((FLAT, SEQS), BF16),
            jax.ShapeDtypeStruct((SENT, SEQS), BF16),
        ],
        scratch_shapes=[
            pltpu.VMEM((SEQS * ROWS, 128), F32),
            pltpu.VMEM((SEQS * ROWS, 128), F32),
            pltpu.VMEM((2 * WIDTH, channels), F32),
            pltpu.VMEM((3, WIDTH, 128), F32),
            pltpu.VMEM((FLAT, 128), F32),
            pltpu.VMEM((FLAT, 128), F32),
        ],
        compiler_params=pltpu.CompilerParams(vmem_limit_bytes=40 << 20),
        cost_estimate=pl.CostEstimate(
            flops=2 * 6144 * 256 * 64, bytes_accessed=4 << 20, transcendentals=6144
        ),
        name="project",
    )(
        depth,
        lines,
        scale.reshape(1, -1),
        shift.reshape(1, -1),
        first,
        first_bias.reshape(1, -1),
        other,
        other_bias.reshape(1, -1),
    )


def tiles_kernel(count, fresh, *refs):
    place_ref, depth_ref, left_ref, *rest = refs
    right_refs, rest = rest[:count], rest[count:]
    final_ref, bias_ref, couple_ref, *rest = rest
    if not fresh:
        rest = rest[1:]
    out_ref, couple_buf, out_buf, take_sem, give_sem = rest

    def columns(b):
        return pl.ds(pl.multiple_of(place_ref[b] * ROWS, 8), ROWS)

    takes, gives = [], []
    for b in range(count):
        takes.append(
            pltpu.make_async_copy(couple_ref.at[:, columns(b), :], couple_buf.at[b], take_sem.at[b])
        )
        gives.append(
            pltpu.make_async_copy(out_buf.at[b], out_ref.at[:, columns(b), :], give_sem.at[b])
        )
        takes[-1].start()

    group = lax.broadcasted_iota(jnp.int32, (144, 128), 1) // WIDTH
    odd = (group & 1) == 1
    upper = (group & 2) == 2
    bias = bias_ref[...]

    def left_turned(k):
        return jnp.concatenate(
            [
                left_ref[(4 * h + (g ^ k)) * WIDTH : (4 * h + (g ^ k) + 1) * WIDTH, :]
                for h in range(6)
                for g in range(4)
            ],
            axis=0,
        )

    def final_turned(v):
        return jnp.concatenate(
            [
                final_ref[(4 * q + (g ^ v)) * WIDTH : (4 * q + (g ^ v) + 1) * WIDTH, :]
                for q in range(8)
                for g in range(4)
            ],
            axis=0,
        )

    for b in range(count):
        right = right_refs[b]
        parts = []
        for k in range(4):
            outer = lax.dot_general(
                right[k * 192 : (k + 1) * 192, :],
                left_turned(k),
                NT,
                preferred_element_type=F32,
            )
            parts.append(
                [
                    jnp.concatenate(
                        [
                            outer[q * ROWS : (q + 1) * ROWS, h * 128 : (h + 1) * 128]
                            for h in range(6)
                        ],
                        axis=0,
                    ).astype(BF16)
                    for q in range(8)
                ]
            )
        mixed = [[], [], [], []]
        for q in range(8):
            pair = [jnp.where(odd, parts[k ^ 1][q], parts[k][q]) for k in range(4)]
            for v in range(4):
                mixed[v].append(jnp.where(upper, pair[v ^ 2], pair[v]))
        depth_row = right[FLAT : FLAT + 16, :128].astype(F32)[:1, :]
        depth_cols = jnp.broadcast_to(as_column(depth_row, ROWS), (ROWS, 128))
        takes[b].wait()
        inside = place_ref[count + b].astype(F32)
        for v in range(4):
            sums = jnp.dot(
                jnp.concatenate(mixed[v], axis=1), final_turned(v), preferred_element_type=F32
            )
            for h in range(6):
                i = 4 * h + v
                pairs = jnp.maximum(jnp.minimum(depth_cols, depth_ref[i].astype(F32)), 1.0)
                update = (sums[h * ROWS : (h + 1) * ROWS] + bias) * (inside / pairs)
                out_buf[b, i] = couple_buf[b, i] + update
        gives[b].start()
    for b in range(count):
        gives[b].wait()


def form_tiles(places, depth, left, rights, final, final_bias, couple, out, name):
    count = len(rights)
    fresh = out is None
    vmem = pl.BlockSpec(memory_space=pltpu.VMEM)
    smem = pl.BlockSpec(memory_space=pltpu.SMEM)
    hbm = pl.BlockSpec(memory_space=pl.ANY)
    args = [places, depth, left, *rights, final, final_bias, couple]
    specs = [smem, smem, vmem] + [vmem] * count + [vmem, vmem, hbm]
    alias = {}
    if not fresh:
        alias = {len(args): 0}
        args.append(out)
        specs.append(hbm)
    return pl.pallas_call(
        functools.partial(tiles_kernel, count, fresh),
        in_specs=specs,
        out_specs=hbm,
        out_shape=jax.ShapeDtypeStruct(couple.shape, couple.dtype),
        input_output_aliases=alias,
        scratch_shapes=[
            pltpu.VMEM((count, ROWS, ROWS, 128), F32),
            pltpu.VMEM((count, ROWS, ROWS, 128), F32),
            pltpu.SemaphoreType.DMA((count,)),
            pltpu.SemaphoreType.DMA((count,)),
        ],
        compiler_params=pltpu.CompilerParams(vmem_limit_bytes=48 << 20),
        cost_estimate=pl.CostEstimate(
            flops=count * 2 * 576 * 1024 * (256 + 128),
            bytes_accessed=count * (2 * 294912 + 401408) + 700000,
            transcendentals=0,
        ),
        name=name,
    )(*args)


def on_device(
    homolog_features,
    standardize_scale,
    standardize_shift,
    first_map_matrix,
    first_map_intercept,
    other_map_matrix,
    other_map_intercept,
    final_map_matrix,
    final_map_intercept,
    coverage_lengths,
    couple_features,
):
    total = lax.axis_size("res")
    me = lax.axis_index("res")
    core = me % 2
    side = 1 - 2 * core

    def moved(block, by):
        return lax.ppermute(block, "res", [(i, (i + by) % total) for i in range(total)])

    def swapped(block):
        return lax.ppermute(block, "res", [(i, i ^ 1) for i in range(total)])

    left, own = project(
        homolog_features,
        coverage_lengths,
        standardize_scale,
        standardize_shift,
        first_map_matrix,
        first_map_intercept,
        other_map_matrix,
        other_map_intercept,
    )
    final = (
        final_map_matrix.reshape(WIDTH, WIDTH, -1).transpose(1, 0, 2).reshape(WIDTH * WIDTH, -1)
    )
    final_bias = final_map_intercept.reshape(1, -1)

    def tiles(distances, rights, out, name):
        at = jnp.stack([jnp.int32(d) + jnp.zeros((), jnp.int32) for d in distances])
        block = me + at
        inside = ((block >= 0) & (block < total)).astype(jnp.int32)
        places = jnp.concatenate([at + WIN, inside])
        return form_tiles(
            places, coverage_lengths, left, rights, final, final_bias, couple_features, out, name
        )

    below2 = moved(own, 2)
    above2 = moved(own, -2)
    sibling = swapped(own)
    out = tiles([0, side], [own, sibling], None, "near")
    below4 = moved(below2, 2)
    above4 = moved(above2, -2)
    below_odd = swapped(below2)
    above_odd = swapped(above2)
    out = tiles([-2, 2, side - 2, side + 2], [below2, above2, below_odd, above_odd], out, "middle")
    last = swapped(jnp.where(core == 0, above4, below4))
    out = tiles([-4, 4], [below4, above4], out, "far")
    return tiles([-3 * side], [last], out, "last")


def solution(mesh):
    return jax.shard_map(
        on_device,
        mesh=mesh,
        in_specs=(
            P(None, "res", None),
            P(),
            P(),
            P(),
            P(),
            P(),
            P(),
            P(),
            P(),
            P("res"),
            P("res", None, None),
        ),
        out_specs=P("res", None, None),
        check_vma=False,
    )
```

```python
import functools

import jax
import jax.numpy as jnp
from jax import lax
from jax.experimental import pallas as pl
from jax.experimental.pallas import tpu as pltpu
from jax.sharding import PartitionSpec as P

WIN = 4
ROWS = 24
WIDTH = 32
SEQS = 256
STEP = 32
PART = 32
FLAT = ROWS * WIDTH
SENT = FLAT + 16

PROJECT_VMEM = 60 << 20
TILES_VMEM = 44 << 20

BF16 = jnp.bfloat16
F32 = jnp.float32
NT = (((1,), (1,)), ((), ()))


def as_column(row, count):
    width = row.shape[1]
    wide = jnp.broadcast_to(row, (count, width))
    at = lax.broadcasted_iota(jnp.int32, (count, width), 1)
    down = lax.broadcasted_iota(jnp.int32, (count, width), 0)
    return jnp.sum(jnp.where(at == down, wide, 0.0), axis=1, keepdims=True)


HBM = pl.BlockSpec(memory_space=pltpu.HBM)
VMEM = pl.BlockSpec(memory_space=pltpu.VMEM)


def start_all(sources, targets, sems):
    copies = [
        pltpu.make_async_copy(source, target, sems.at[n])
        for n, (source, target) in enumerate(zip(sources, targets))
    ]
    for copy in copies:
        copy.start()
    return copies


def project_kernel(
    depth_hbm,
    lines_hbm,
    scale_hbm,
    shift_hbm,
    first_hbm,
    first_bias_hbm,
    other_hbm,
    other_bias_hbm,
    left_ref,
    right_ref,
    depth_ref,
    lines_ref,
    scale_ref,
    shift_ref,
    first_ref,
    first_bias_ref,
    other_ref,
    other_bias_ref,
    low_ref,
    high_ref,
    maps_ref,
    turn_ref,
    right_low_ref,
    right_high_ref,
    lines_sem,
    small_sem,
):
    steps = SEQS // STEP

    def fetch(s):
        at = pl.ds(pl.multiple_of(s * STEP, STEP), STEP)
        return pltpu.make_async_copy(lines_hbm.at[at], lines_ref.at[at], lines_sem.at[s])

    fetch(0).start()
    small = start_all(
        (scale_hbm, shift_hbm, first_hbm, first_bias_hbm, other_hbm, other_bias_hbm, depth_hbm),
        (scale_ref, shift_ref, first_ref, first_bias_ref, other_ref, other_bias_ref, depth_ref),
        small_sem,
    )
    for s in range(1, steps):
        fetch(s).start()
    for copy in small:
        copy.wait()

    maps_ref[:WIDTH, :] = first_ref[...].astype(F32)
    turned = other_ref[...].astype(F32)
    first_bias = as_column(first_bias_ref[...], WIDTH)
    other_bias = jnp.broadcast_to(as_column(other_bias_ref[...], WIDTH), (WIDTH, 128))
    turn_ref[0] = turned[:, :128]
    turn_ref[1] = turned[:, 128:]
    turn_ref[2] = other_bias
    biases = [jnp.broadcast_to(first_bias, (WIDTH, 128))]
    for k in range(4):
        for half in range(2):
            maps_ref[WIDTH + 8 * k : WIDTH + 8 * k + 8, half * 128 : half * 128 + 128] = turn_ref[
                half, pl.ds(k, 8, stride=4), :
            ]
        biases.append(turn_ref[2, pl.ds(k, 8, stride=4), :])
    bias = jnp.concatenate(biases, axis=0)
    bias = jnp.concatenate([bias, bias], axis=1)
    maps = maps_ref[...].astype(BF16)
    scale = scale_ref[...]
    shift = shift_ref[...]

    def normalise(s, carry):
        fetch(s).wait()
        for c in range(STEP // PART):
            at = pl.ds(pl.multiple_of(s * STEP + c * PART, PART), PART)
            x = lines_ref[at].astype(F32).reshape(PART * ROWS, -1)
            centred = x - jnp.mean(x, axis=1, keepdims=True)
            variance = jnp.mean(centred * centred, axis=1, keepdims=True)
            normed = centred * lax.rsqrt(variance + 1e-05) * scale + shift
            at = pl.ds(pl.multiple_of((s * STEP + c * PART) * ROWS, 8), PART * ROWS)
            low_ref[at, :] = normed[:, :128]
            high_ref[at, :] = normed[:, 128:]
        return carry

    lax.fori_loop(0, steps, normalise, 0)

    seq = lax.broadcasted_iota(jnp.int32, (2 * WIDTH, SEQS), 1)
    lane = lax.broadcasted_iota(jnp.int32, (16, SEQS), 1)
    depths = jnp.zeros((16, SEQS), F32)
    for i in range(ROWS):
        depth = depth_ref[i]
        rows = jnp.concatenate(
            [low_ref[pl.ds(i, SEQS, stride=ROWS), :], high_ref[pl.ds(i, SEQS, stride=ROWS), :]],
            axis=1,
        ).astype(BF16)
        both = lax.dot_general(maps, rows, NT, preferred_element_type=F32) + bias
        both = jnp.where(seq < depth, both, 0.0)
        left_ref[i * WIDTH : (i + 1) * WIDTH, :] = both[:WIDTH].astype(BF16)
        right_low_ref[pl.ds(i, WIDTH, stride=ROWS), :] = both[WIDTH:, :128]
        right_high_ref[pl.ds(i, WIDTH, stride=ROWS), :] = both[WIDTH:, 128:]
        depths = jnp.where(lane == i, depth.astype(F32), depths)
    right_ref[:FLAT, :128] = right_low_ref[...].astype(BF16)
    right_ref[:FLAT, 128:] = right_high_ref[...].astype(BF16)
    right_ref[FLAT:, :] = depths.astype(BF16)


def project(lines, depth, scale, shift, first, first_bias, other, other_bias):
    channels = lines.shape[2]
    return pl.pallas_call(
        project_kernel,
        in_specs=[HBM] * 8,
        out_specs=[VMEM] * 2,
        out_shape=[
            jax.ShapeDtypeStruct((FLAT, SEQS), BF16),
            jax.ShapeDtypeStruct((SENT, SEQS), BF16),
        ],
        scratch_shapes=[
            pltpu.SMEM((ROWS,), jnp.int32),
            pltpu.VMEM((SEQS, ROWS, channels), BF16),
            pltpu.VMEM((1, channels), F32),
            pltpu.VMEM((1, channels), F32),
            pltpu.VMEM((WIDTH, channels), BF16),
            pltpu.VMEM((1, WIDTH), F32),
            pltpu.VMEM((WIDTH, channels), BF16),
            pltpu.VMEM((1, WIDTH), F32),
            pltpu.VMEM((SEQS * ROWS, 128), F32),
            pltpu.VMEM((SEQS * ROWS, 128), F32),
            pltpu.VMEM((2 * WIDTH, channels), F32),
            pltpu.VMEM((3, WIDTH, 128), F32),
            pltpu.VMEM((FLAT, 128), F32),
            pltpu.VMEM((FLAT, 128), F32),
            pltpu.SemaphoreType.DMA((SEQS // STEP,)),
            pltpu.SemaphoreType.DMA((7,)),
        ],
        compiler_params=pltpu.CompilerParams(vmem_limit_bytes=PROJECT_VMEM),
        cost_estimate=pl.CostEstimate(
            flops=2 * 6144 * 256 * 64, bytes_accessed=4 << 20, transcendentals=6144
        ),
        name="project",
    )(
        depth,
        lines,
        scale.reshape(1, -1),
        shift.reshape(1, -1),
        first.T,
        first_bias.reshape(1, -1),
        other.T,
        other_bias.reshape(1, -1),
    )


def tiles_kernel(distances, either, fresh, total, *refs):
    count = len(distances)
    me = lax.axis_index("res")
    side = 1 - 2 * (me % 2)
    depth_hbm, left_ref, *rest = refs
    given = count + int(either)
    right_refs, rest = rest[:given], rest[given:]
    final_in, bias_hbm, couple_hbm, *rest = rest
    if fresh:
        out_hbm, final_ref, *rest = rest
        *rest, final_raw, final_wide = rest
    else:
        final_ref = final_in
        _, out_hbm, *rest = rest
    (
        depth_ref,
        bias_ref,
        picked_ref,
        couple_buf,
        out_buf,
        small_sem,
        take_sem,
        give_sem,
    ) = rest
    blocks = [me + by(side) for by in distances]

    def columns(b):
        place = jnp.clip(blocks[b] - me + WIN, 0, 2 * WIN)
        return pl.ds(pl.multiple_of(place * ROWS, 8), ROWS)

    if fresh:
        final_take = pltpu.make_async_copy(final_in, final_raw, small_sem.at[2])
        final_take.start()
    small = start_all((depth_hbm, bias_hbm), (depth_ref, bias_ref), small_sem)
    takes = start_all(
        [couple_hbm.at[:, :, columns(b), :] for b in range(count)],
        [couple_buf.at[b] for b in range(count)],
        take_sem,
    )
    gives = [
        [
            pltpu.make_async_copy(
                out_buf.at[b, v], out_hbm.at[:, v, columns(b), :], give_sem.at[b, v]
            )
            for b in range(count)
        ]
        for v in range(4)
    ]
    if fresh:
        final_take.wait()
        final_wide[...] = final_raw[...].astype(F32)
        for y in range(0, WIDTH, 2):
            final_ref[y * WIDTH : (y + 2) * WIDTH, :] = jnp.concatenate(
                [final_wide[pl.ds(y + o, WIDTH, stride=WIDTH), :] for o in range(2)], axis=0
            ).astype(BF16)
    for copy in small:
        copy.wait()
    if either:
        picked_ref[...] = jnp.where(side > 0, right_refs[-2][...], right_refs[-1][...])
        right_refs = [*right_refs[:-2], picked_ref]

    group = lax.broadcasted_iota(jnp.int32, (count * 144, 128), 1) // WIDTH
    odd = (group & 1) == 1
    upper = (group & 2) == 2
    bias = bias_ref[...]

    def turned(ref, parts, k):
        return jnp.concatenate(
            [
                ref[(4 * p + (g ^ k)) * WIDTH : (4 * p + (g ^ k) + 1) * WIDTH, :]
                for p in range(parts)
                for g in range(4)
            ],
            axis=0,
        )

    parts = []
    for k in range(4):
        outer = lax.dot_general(
            jnp.concatenate([right[k * 192 : (k + 1) * 192, :] for right in right_refs], axis=0),
            turned(left_ref, 6, k),
            NT,
            preferred_element_type=F32,
        )
        parts.append(
            [
                jnp.concatenate(
                    [
                        outer[
                            b * 192 + q * ROWS : b * 192 + (q + 1) * ROWS, h * 128 : (h + 1) * 128
                        ]
                        for b in range(count)
                        for h in range(6)
                    ],
                    axis=0,
                ).astype(BF16)
                for q in range(8)
            ]
        )
    mixed = [[], [], [], []]
    for q in range(8):
        pair = [jnp.where(odd, parts[k ^ 1][q], parts[k][q]) for k in range(4)]
        for v in range(4):
            mixed[v].append(jnp.where(upper, pair[v ^ 2], pair[v]))
    shares = []
    for b in range(count):
        depth_row = right_refs[b][FLAT : FLAT + 16, :128].astype(F32)[:1, :]
        depth_cols = jnp.broadcast_to(as_column(depth_row, ROWS), (ROWS, 128))
        inside = ((blocks[b] >= 0) & (blocks[b] < total)).astype(F32)
        shares.append((depth_cols, inside))
    for v in range(4):
        sums = jnp.dot(
            jnp.concatenate(mixed[v], axis=1),
            turned(final_ref, 8, v),
            preferred_element_type=F32,
        )
        for b in range(count):
            if v == 0:
                takes[b].wait()
            depth_cols, inside = shares[b]
            for h in range(6):
                depth = depth_ref[4 * h + v].astype(F32)
                pairs = jnp.maximum(jnp.minimum(depth_cols, depth), 1.0)
                update = sums[(b * 6 + h) * ROWS : (b * 6 + h + 1) * ROWS] + bias
                out_buf[b, v, h] = couple_buf[b, h, v] + update * (inside / pairs)
            gives[v][b].start()
    for copies in gives:
        for copy in copies:
            copy.wait()


def form_tiles(distances, either, total, depth, left, rights, final, final_bias, couple, out, name):
    count = len(distances)
    fresh = out is None
    args = [depth, left, *rights, final, final_bias, couple]
    specs = [HBM, VMEM] + [VMEM] * len(rights) + [HBM if fresh else VMEM, HBM, HBM]
    alias = {}
    out_specs = [HBM]
    out_shape = [jax.ShapeDtypeStruct(couple.shape, couple.dtype)]
    extra = []
    if fresh:
        out_specs.append(VMEM)
        out_shape.append(jax.ShapeDtypeStruct(final.shape, final.dtype))
        extra = [pltpu.VMEM(final.shape, BF16), pltpu.VMEM(final.shape, F32)]
    else:
        alias = {len(args): 0}
        args.append(out)
        specs.append(HBM)
    return pl.pallas_call(
        functools.partial(tiles_kernel, distances, either, fresh, total),
        in_specs=specs,
        out_specs=out_specs,
        out_shape=out_shape,
        input_output_aliases=alias,
        scratch_shapes=[
            pltpu.SMEM((ROWS,), jnp.int32),
            pltpu.VMEM((1, 128), F32),
            pltpu.VMEM((SENT, SEQS), BF16),
            pltpu.VMEM((count, 6, 4, ROWS, 128), F32),
            pltpu.VMEM((count, 4, 6, ROWS, 128), F32),
            pltpu.SemaphoreType.DMA((3,)),
            pltpu.SemaphoreType.DMA((count,)),
            pltpu.SemaphoreType.DMA((count, 4)),
            *extra,
        ],
        compiler_params=pltpu.CompilerParams(vmem_limit_bytes=TILES_VMEM),
        cost_estimate=pl.CostEstimate(
            flops=count, bytes_accessed=count, transcendentals=0
        ),
        name=name,
    )(*args)


def on_device(
    homolog_features,
    standardize_scale,
    standardize_shift,
    first_map_matrix,
    first_map_intercept,
    other_map_matrix,
    other_map_intercept,
    final_map_matrix,
    final_map_intercept,
    coverage_lengths,
    couple_features,
):
    total = lax.axis_size("res")
    def moved(block, by):
        return lax.ppermute(block, "res", [(i, (i + by) % total) for i in range(total)])

    def swapped(block):
        return lax.ppermute(block, "res", [(i, i ^ 1) for i in range(total)])

    left, own = project(
        homolog_features,
        coverage_lengths,
        standardize_scale,
        standardize_shift,
        first_map_matrix,
        first_map_intercept,
        other_map_matrix,
        other_map_intercept,
    )
    final_bias = final_map_intercept.reshape(1, -1)

    def tiles(distances, rights, final, out, name, either=False):
        return form_tiles(
            distances,
            either,
            total,
            coverage_lengths,
            left,
            rights,
            final,
            final_bias,
            couple,
            out,
            name,
        )

    couple = couple_features.reshape(ROWS // 4, 4, *couple_features.shape[1:])
    below = moved(own, 2)
    above = moved(own, -2)
    sibling = swapped(own)
    out, final = tiles(
        [lambda side: 0, lambda side: side],
        [own, sibling],
        final_map_matrix,
        None,
        "near",
    )
    below, above, out = lax.optimization_barrier((below, above, out))
    below_far = moved(below, 2)
    above_far = moved(above, -2)
    below_odd = swapped(below)
    above_odd = swapped(above)
    (out,) = tiles(
        [
            lambda side: -2,
            lambda side: 2,
            lambda side: side - 2,
            lambda side: side + 2,
        ],
        [below, above, below_odd, above_odd],
        final,
        out,
        "middle",
    )
    below_far, above_far, out = lax.optimization_barrier((below_far, above_far, out))
    below_far_odd = swapped(below_far)
    above_far_odd = swapped(above_far)
    (out,) = tiles(
        [
            lambda side: -4,
            lambda side: 4,
            lambda side: -3 * side,
        ],
        [below_far, above_far, below_far_odd, above_far_odd],
        final,
        out,
        "far",
        either=True,
    )
    return out.reshape(couple_features.shape)


def solution(mesh):
    return jax.shard_map(
        on_device,
        mesh=mesh,
        in_specs=(
            P(None, "res", None),
            P(),
            P(),
            P(),
            P(),
            P(),
            P(),
            P(),
            P(),
            P("res"),
            P("res", None, None),
        ),
        out_specs=P("res", None, None),
        check_vma=False,
    )
```

```python
import functools

import jax
import jax.numpy as jnp
from jax import lax
from jax.experimental import pallas as pl
from jax.experimental.pallas import tpu as pltpu
from jax.sharding import PartitionSpec as P

WIN = 4
ROWS = 24
WIDTH = 32
SEQS = 256
STEP = 64
PART = 64
FLAT = ROWS * WIDTH
SENT = FLAT + 16

PROJECT_VMEM = 60 << 20
TILES_VMEM = 44 << 20

BF16 = jnp.bfloat16
F32 = jnp.float32
NT = (((1,), (1,)), ((), ()))


def as_column(row, count):
    width = row.shape[1]
    wide = jnp.broadcast_to(row, (count, width))
    at = lax.broadcasted_iota(jnp.int32, (count, width), 1)
    down = lax.broadcasted_iota(jnp.int32, (count, width), 0)
    return jnp.sum(jnp.where(at == down, wide, 0.0), axis=1, keepdims=True)


HBM = pl.BlockSpec(memory_space=pltpu.HBM)
VMEM = pl.BlockSpec(memory_space=pltpu.VMEM)


def start_all(sources, targets, sems):
    copies = [
        pltpu.make_async_copy(source, target, sems.at[n])
        for n, (source, target) in enumerate(zip(sources, targets))
    ]
    for copy in copies:
        copy.start()
    return copies


def project_kernel(
    depth_hbm,
    lines_hbm,
    scale_hbm,
    shift_hbm,
    first_hbm,
    first_bias_hbm,
    other_hbm,
    other_bias_hbm,
    left_ref,
    right_ref,
    depth_ref,
    lines_ref,
    scale_ref,
    shift_ref,
    first_ref,
    first_bias_ref,
    other_ref,
    other_bias_ref,
    low_ref,
    high_ref,
    maps_ref,
    turn_ref,
    right_low_ref,
    right_high_ref,
    lines_sem,
    small_sem,
):
    steps = SEQS // STEP

    def fetch(s):
        at = pl.ds(pl.multiple_of(s * STEP, STEP), STEP)
        return pltpu.make_async_copy(lines_hbm.at[at], lines_ref.at[at], lines_sem.at[s])

    fetch(0).start()
    small = start_all(
        (scale_hbm, shift_hbm, first_hbm, first_bias_hbm, other_hbm, other_bias_hbm, depth_hbm),
        (scale_ref, shift_ref, first_ref, first_bias_ref, other_ref, other_bias_ref, depth_ref),
        small_sem,
    )
    for s in range(1, steps):
        fetch(s).start()
    for copy in small:
        copy.wait()

    maps_ref[:WIDTH, :] = first_ref[...].astype(F32)
    turned = other_ref[...].astype(F32)
    first_bias = as_column(first_bias_ref[...], WIDTH)
    other_bias = jnp.broadcast_to(as_column(other_bias_ref[...], WIDTH), (WIDTH, 128))
    turn_ref[0] = turned[:, :128]
    turn_ref[1] = turned[:, 128:]
    turn_ref[2] = other_bias
    biases = [jnp.broadcast_to(first_bias, (WIDTH, 128))]
    for k in range(4):
        for half in range(2):
            maps_ref[WIDTH + 8 * k : WIDTH + 8 * k + 8, half * 128 : half * 128 + 128] = turn_ref[
                half, pl.ds(k, 8, stride=4), :
            ]
        biases.append(turn_ref[2, pl.ds(k, 8, stride=4), :])
    bias = jnp.concatenate(biases, axis=0)
    bias = jnp.concatenate([bias, bias], axis=1)
    maps = maps_ref[...].astype(BF16)
    scale = scale_ref[...]
    shift = shift_ref[...]

    def normalise(s, carry):
        fetch(s).wait()
        for c in range(STEP // PART):
            at = pl.ds(pl.multiple_of(s * STEP + c * PART, PART), PART)
            x = lines_ref[at].astype(F32).reshape(PART * ROWS, -1)
            centred = x - jnp.mean(x, axis=1, keepdims=True)
            variance = jnp.mean(centred * centred, axis=1, keepdims=True)
            normed = centred * lax.rsqrt(variance + 1e-05) * scale + shift
            at = pl.ds(pl.multiple_of((s * STEP + c * PART) * ROWS, 8), PART * ROWS)
            low_ref[at, :] = normed[:, :128]
            high_ref[at, :] = normed[:, 128:]
        return carry

    lax.fori_loop(0, steps, normalise, 0)

    seq = lax.broadcasted_iota(jnp.int32, (2 * WIDTH, SEQS), 1)
    lane = lax.broadcasted_iota(jnp.int32, (16, SEQS), 1)
    depths = jnp.zeros((16, SEQS), F32)
    for i in range(ROWS):
        depth = depth_ref[i]
        rows = jnp.concatenate(
            [low_ref[pl.ds(i, SEQS, stride=ROWS), :], high_ref[pl.ds(i, SEQS, stride=ROWS), :]],
            axis=1,
        ).astype(BF16)
        both = lax.dot_general(maps, rows, NT, preferred_element_type=F32) + bias
        both = jnp.where(seq < depth, both, 0.0)
        left_ref[i * WIDTH : (i + 1) * WIDTH, :] = both[:WIDTH].astype(BF16)
        right_low_ref[pl.ds(i, WIDTH, stride=ROWS), :] = both[WIDTH:, :128]
        right_high_ref[pl.ds(i, WIDTH, stride=ROWS), :] = both[WIDTH:, 128:]
        depths = jnp.where(lane == i, depth.astype(F32), depths)
    right_ref[:FLAT, :128] = right_low_ref[...].astype(BF16)
    right_ref[:FLAT, 128:] = right_high_ref[...].astype(BF16)
    right_ref[FLAT:, :] = depths.astype(BF16)


def project(lines, depth, scale, shift, first, first_bias, other, other_bias):
    channels = lines.shape[2]
    return pl.pallas_call(
        project_kernel,
        in_specs=[HBM] * 8,
        out_specs=[VMEM] * 2,
        out_shape=[
            jax.ShapeDtypeStruct((FLAT, SEQS), BF16),
            jax.ShapeDtypeStruct((SENT, SEQS), BF16),
        ],
        scratch_shapes=[
            pltpu.SMEM((ROWS,), jnp.int32),
            pltpu.VMEM((SEQS, ROWS, channels), BF16),
            pltpu.VMEM((1, channels), F32),
            pltpu.VMEM((1, channels), F32),
            pltpu.VMEM((WIDTH, channels), BF16),
            pltpu.VMEM((1, WIDTH), F32),
            pltpu.VMEM((WIDTH, channels), BF16),
            pltpu.VMEM((1, WIDTH), F32),
            pltpu.VMEM((SEQS * ROWS, 128), F32),
            pltpu.VMEM((SEQS * ROWS, 128), F32),
            pltpu.VMEM((2 * WIDTH, channels), F32),
            pltpu.VMEM((3, WIDTH, 128), F32),
            pltpu.VMEM((FLAT, 128), F32),
            pltpu.VMEM((FLAT, 128), F32),
            pltpu.SemaphoreType.DMA((SEQS // STEP,)),
            pltpu.SemaphoreType.DMA((7,)),
        ],
        compiler_params=pltpu.CompilerParams(vmem_limit_bytes=PROJECT_VMEM),
        cost_estimate=pl.CostEstimate(
            flops=2 * 6144 * 256 * 64, bytes_accessed=4 << 20, transcendentals=6144
        ),
        name="project",
    )(
        depth,
        lines,
        scale.reshape(1, -1),
        shift.reshape(1, -1),
        first.T,
        first_bias.reshape(1, -1),
        other.T,
        other_bias.reshape(1, -1),
    )


def tiles_kernel(distances, either, fresh, total, *refs):
    count = len(distances)
    me = lax.axis_index("res")
    side = 1 - 2 * (me % 2)
    depth_hbm, left_ref, *rest = refs
    given = count + int(either)
    right_refs, rest = rest[:given], rest[given:]
    final_in, bias_hbm, couple_hbm, *rest = rest
    if fresh:
        out_hbm, final_ref, *rest = rest
        *rest, final_raw, final_wide = rest
    else:
        final_ref = final_in
        _, out_hbm, *rest = rest
    (
        depth_ref,
        bias_ref,
        picked_ref,
        couple_buf,
        out_buf,
        small_sem,
        take_sem,
        give_sem,
    ) = rest
    blocks = [me + by(side) for by in distances]

    def columns(b):
        place = jnp.clip(blocks[b] - me + WIN, 0, 2 * WIN)
        return pl.ds(pl.multiple_of(place * ROWS, 8), ROWS)

    if fresh:
        final_take = pltpu.make_async_copy(final_in, final_raw, small_sem.at[2])
        final_take.start()
    small = start_all((depth_hbm, bias_hbm), (depth_ref, bias_ref), small_sem)
    takes = start_all(
        [couple_hbm.at[:, :, columns(b), :] for b in range(count)],
        [couple_buf.at[b] for b in range(count)],
        take_sem,
    )
    gives = [
        [
            pltpu.make_async_copy(
                out_buf.at[b, v], out_hbm.at[:, v, columns(b), :], give_sem.at[b, v]
            )
            for b in range(count)
        ]
        for v in range(4)
    ]
    if fresh:
        final_take.wait()
        final_wide[...] = final_raw[...].astype(F32)
        for y in range(0, WIDTH, 2):
            final_ref[y * WIDTH : (y + 2) * WIDTH, :] = jnp.concatenate(
                [final_wide[pl.ds(y + o, WIDTH, stride=WIDTH), :] for o in range(2)], axis=0
            ).astype(BF16)
    if either:
        picked_ref[...] = jnp.where(side > 0, right_refs[-2][...], right_refs[-1][...])
        right_refs = [*right_refs[:-2], picked_ref]

    group = lax.broadcasted_iota(jnp.int32, (count * 144, 128), 1) // WIDTH
    odd = (group & 1) == 1
    upper = (group & 2) == 2

    def turned(ref, parts, k):
        return jnp.concatenate(
            [
                ref[(4 * p + (g ^ k)) * WIDTH : (4 * p + (g ^ k) + 1) * WIDTH, :]
                for p in range(parts)
                for g in range(4)
            ],
            axis=0,
        )

    parts = []
    for k in range(4):
        outer = lax.dot_general(
            jnp.concatenate([right[k * 192 : (k + 1) * 192, :] for right in right_refs], axis=0),
            turned(left_ref, 6, k),
            NT,
            preferred_element_type=F32,
        )
        parts.append(
            [
                jnp.concatenate(
                    [
                        outer[
                            b * 192 + q * ROWS : b * 192 + (q + 1) * ROWS, h * 128 : (h + 1) * 128
                        ]
                        for b in range(count)
                        for h in range(6)
                    ],
                    axis=0,
                ).astype(BF16)
                for q in range(8)
            ]
        )
    mixed = [[], [], [], []]
    for q in range(8):
        pair = [jnp.where(odd, parts[k ^ 1][q], parts[k][q]) for k in range(4)]
        for v in range(4):
            mixed[v].append(jnp.where(upper, pair[v ^ 2], pair[v]))
    shares = []
    for b in range(count):
        depth_row = right_refs[b][FLAT : FLAT + 16, :128].astype(F32)[:1, :]
        depth_cols = jnp.broadcast_to(as_column(depth_row, ROWS), (ROWS, 128))
        inside = ((blocks[b] >= 0) & (blocks[b] < total)).astype(F32)
        shares.append((depth_cols, inside))
    for copy in small:
        copy.wait()
    bias = bias_ref[...]
    for v in range(4):
        sums = jnp.dot(
            jnp.concatenate(mixed[v], axis=1),
            turned(final_ref, 8, v),
            preferred_element_type=F32,
        )
        for b in range(count):
            if v == 0:
                takes[b].wait()
            depth_cols, inside = shares[b]
            for h in range(6):
                depth = depth_ref[4 * h + v].astype(F32)
                pairs = jnp.maximum(jnp.minimum(depth_cols, depth), 1.0)
                update = sums[(b * 6 + h) * ROWS : (b * 6 + h + 1) * ROWS] + bias
                out_buf[b, v, h] = couple_buf[b, h, v] + update * (inside / pairs)
            gives[v][b].start()
    for copies in gives:
        for copy in copies:
            copy.wait()


def form_tiles(distances, either, total, depth, left, rights, final, final_bias, couple, out, name):
    count = len(distances)
    fresh = out is None
    args = [depth, left, *rights, final, final_bias, couple]
    specs = [HBM, VMEM] + [VMEM] * len(rights) + [HBM if fresh else VMEM, HBM, HBM]
    alias = {}
    out_specs = [HBM]
    out_shape = [jax.ShapeDtypeStruct(couple.shape, couple.dtype)]
    extra = []
    if fresh:
        out_specs.append(VMEM)
        out_shape.append(jax.ShapeDtypeStruct(final.shape, final.dtype))
        extra = [pltpu.VMEM(final.shape, BF16), pltpu.VMEM(final.shape, F32)]
    else:
        alias = {len(args): 0}
        args.append(out)
        specs.append(HBM)
    return pl.pallas_call(
        functools.partial(tiles_kernel, distances, either, fresh, total),
        in_specs=specs,
        out_specs=out_specs,
        out_shape=out_shape,
        input_output_aliases=alias,
        scratch_shapes=[
            pltpu.SMEM((ROWS,), jnp.int32),
            pltpu.VMEM((1, 128), F32),
            pltpu.VMEM((SENT, SEQS), BF16),
            pltpu.VMEM((count, 6, 4, ROWS, 128), F32),
            pltpu.VMEM((count, 4, 6, ROWS, 128), F32),
            pltpu.SemaphoreType.DMA((3,)),
            pltpu.SemaphoreType.DMA((count,)),
            pltpu.SemaphoreType.DMA((count, 4)),
            *extra,
        ],
        compiler_params=pltpu.CompilerParams(vmem_limit_bytes=TILES_VMEM),
        cost_estimate=pl.CostEstimate(
            flops=count, bytes_accessed=count, transcendentals=0
        ),
        name=name,
    )(*args)


def on_device(
    homolog_features,
    standardize_scale,
    standardize_shift,
    first_map_matrix,
    first_map_intercept,
    other_map_matrix,
    other_map_intercept,
    final_map_matrix,
    final_map_intercept,
    coverage_lengths,
    couple_features,
):
    total = lax.axis_size("res")
    def moved(block, by):
        return lax.ppermute(block, "res", [(i, (i + by) % total) for i in range(total)])

    def swapped(block):
        return lax.ppermute(block, "res", [(i, i ^ 1) for i in range(total)])

    left, own = project(
        homolog_features,
        coverage_lengths,
        standardize_scale,
        standardize_shift,
        first_map_matrix,
        first_map_intercept,
        other_map_matrix,
        other_map_intercept,
    )
    final_bias = final_map_intercept.reshape(1, -1)

    def tiles(distances, rights, final, out, name, either=False):
        return form_tiles(
            distances,
            either,
            total,
            coverage_lengths,
            left,
            rights,
            final,
            final_bias,
            couple,
            out,
            name,
        )

    couple = couple_features.reshape(ROWS // 4, 4, *couple_features.shape[1:])
    below = moved(own, 2)
    above = moved(own, -2)
    sibling = swapped(own)
    out, final = tiles(
        [lambda side: 0, lambda side: side],
        [own, sibling],
        final_map_matrix,
        None,
        "near",
    )
    below, above, out = lax.optimization_barrier((below, above, out))
    below_far = moved(below, 2)
    above_far = moved(above, -2)
    below_odd = swapped(below)
    above_odd = swapped(above)
    (out,) = tiles(
        [
            lambda side: -2,
            lambda side: 2,
            lambda side: side - 2,
            lambda side: side + 2,
        ],
        [below, above, below_odd, above_odd],
        final,
        out,
        "middle",
    )
    below_far, above_far, out = lax.optimization_barrier((below_far, above_far, out))
    below_far_odd = swapped(below_far)
    above_far_odd = swapped(above_far)
    (out,) = tiles([lambda side: -4, lambda side: 4], [below_far, above_far], final, out, "far")
    (out,) = tiles(
        [lambda side: -3 * side],
        [below_far_odd, above_far_odd],
        final,
        out,
        "last",
        either=True,
    )
    return out.reshape(couple_features.shape)


def solution(mesh):
    return jax.shard_map(
        on_device,
        mesh=mesh,
        in_specs=(
            P(None, "res", None),
            P(),
            P(),
            P(),
            P(),
            P(),
            P(),
            P(),
            P(),
            P("res"),
            P("res", None, None),
        ),
        out_specs=P("res", None, None),
        check_vma=False,
    )
```

```python
import functools

import jax
import jax.numpy as jnp
from jax import lax
from jax.experimental import pallas as pl
from jax.experimental.pallas import tpu as pltpu
from jax.sharding import PartitionSpec as P

WIN = 4
ROWS = 24
WIDTH = 32
SEQS = 256
STEP = 64
PART = 32
FLAT = ROWS * WIDTH
SENT = FLAT + 16

PROJECT_VMEM = 60 << 20
TILES_VMEM = 44 << 20

BF16 = jnp.bfloat16
F32 = jnp.float32
NT = (((1,), (1,)), ((), ()))


def as_column(row, count):
    width = row.shape[1]
    wide = jnp.broadcast_to(row, (count, width))
    at = lax.broadcasted_iota(jnp.int32, (count, width), 1)
    down = lax.broadcasted_iota(jnp.int32, (count, width), 0)
    return jnp.sum(jnp.where(at == down, wide, 0.0), axis=1, keepdims=True)


HBM = pl.BlockSpec(memory_space=pltpu.HBM)
VMEM = pl.BlockSpec(memory_space=pltpu.VMEM)


def start_all(sources, targets, sems):
    copies = [
        pltpu.make_async_copy(source, target, sems.at[n])
        for n, (source, target) in enumerate(zip(sources, targets))
    ]
    for copy in copies:
        copy.start()
    return copies


def project_kernel(
    depth_hbm,
    lines_hbm,
    scale_hbm,
    shift_hbm,
    first_hbm,
    first_bias_hbm,
    other_hbm,
    other_bias_hbm,
    left_ref,
    right_ref,
    depth_ref,
    lines_ref,
    scale_ref,
    shift_ref,
    first_ref,
    first_bias_ref,
    other_ref,
    other_bias_ref,
    low_ref,
    high_ref,
    maps_ref,
    turn_ref,
    right_low_ref,
    right_high_ref,
    lines_sem,
    small_sem,
):
    steps = SEQS // STEP

    def fetch(s):
        at = pl.ds(pl.multiple_of(s * STEP, STEP), STEP)
        return pltpu.make_async_copy(lines_hbm.at[at], lines_ref.at[at], lines_sem.at[s])

    fetch(0).start()
    small = start_all(
        (scale_hbm, shift_hbm, first_hbm, first_bias_hbm, other_hbm, other_bias_hbm, depth_hbm),
        (scale_ref, shift_ref, first_ref, first_bias_ref, other_ref, other_bias_ref, depth_ref),
        small_sem,
    )
    for s in range(1, steps):
        fetch(s).start()
    for copy in small:
        copy.wait()

    maps_ref[:WIDTH, :] = first_ref[...].astype(F32)
    turned = other_ref[...].astype(F32)
    first_bias = as_column(first_bias_ref[...], WIDTH)
    other_bias = jnp.broadcast_to(as_column(other_bias_ref[...], WIDTH), (WIDTH, 128))
    turn_ref[0] = turned[:, :128]
    turn_ref[1] = turned[:, 128:]
    turn_ref[2] = other_bias
    biases = [jnp.broadcast_to(first_bias, (WIDTH, 128))]
    for k in range(4):
        for half in range(2):
            maps_ref[WIDTH + 8 * k : WIDTH + 8 * k + 8, half * 128 : half * 128 + 128] = turn_ref[
                half, pl.ds(k, 8, stride=4), :
            ]
        biases.append(turn_ref[2, pl.ds(k, 8, stride=4), :])
    bias = jnp.concatenate(biases, axis=0)
    bias = jnp.concatenate([bias, bias], axis=1)
    maps = maps_ref[...].astype(BF16)
    scale = scale_ref[...]
    shift = shift_ref[...]

    def normalise(s, carry):
        fetch(s).wait()
        for c in range(STEP // PART):
            at = pl.ds(pl.multiple_of(s * STEP + c * PART, PART), PART)
            x = lines_ref[at].astype(F32).reshape(PART * ROWS, -1)
            centred = x - jnp.mean(x, axis=1, keepdims=True)
            variance = jnp.mean(centred * centred, axis=1, keepdims=True)
            normed = centred * lax.rsqrt(variance + 1e-05) * scale + shift
            at = pl.ds(pl.multiple_of((s * STEP + c * PART) * ROWS, 8), PART * ROWS)
            low_ref[at, :] = normed[:, :128]
            high_ref[at, :] = normed[:, 128:]
        return carry

    lax.fori_loop(0, steps, normalise, 0)

    seq = lax.broadcasted_iota(jnp.int32, (2 * WIDTH, SEQS), 1)
    lane = lax.broadcasted_iota(jnp.int32, (16, SEQS), 1)
    depths = jnp.zeros((16, SEQS), F32)
    for i in range(ROWS):
        depth = depth_ref[i]
        rows = jnp.concatenate(
            [low_ref[pl.ds(i, SEQS, stride=ROWS), :], high_ref[pl.ds(i, SEQS, stride=ROWS), :]],
            axis=1,
        ).astype(BF16)
        both = lax.dot_general(maps, rows, NT, preferred_element_type=F32) + bias
        both = jnp.where(seq < depth, both, 0.0)
        left_ref[i * WIDTH : (i + 1) * WIDTH, :] = both[:WIDTH].astype(BF16)
        right_low_ref[pl.ds(i, WIDTH, stride=ROWS), :] = both[WIDTH:, :128]
        right_high_ref[pl.ds(i, WIDTH, stride=ROWS), :] = both[WIDTH:, 128:]
        depths = jnp.where(lane == i, depth.astype(F32), depths)
    right_ref[:FLAT, :128] = right_low_ref[...].astype(BF16)
    right_ref[:FLAT, 128:] = right_high_ref[...].astype(BF16)
    right_ref[FLAT:, :] = depths.astype(BF16)


def project(lines, depth, scale, shift, first, first_bias, other, other_bias):
    channels = lines.shape[2]
    return pl.pallas_call(
        project_kernel,
        in_specs=[HBM] * 8,
        out_specs=[VMEM] * 2,
        out_shape=[
            jax.ShapeDtypeStruct((FLAT, SEQS), BF16),
            jax.ShapeDtypeStruct((SENT, SEQS), BF16),
        ],
        scratch_shapes=[
            pltpu.SMEM((ROWS,), jnp.int32),
            pltpu.VMEM((SEQS, ROWS, channels), BF16),
            pltpu.VMEM((1, channels), F32),
            pltpu.VMEM((1, channels), F32),
            pltpu.VMEM((WIDTH, channels), BF16),
            pltpu.VMEM((1, WIDTH), F32),
            pltpu.VMEM((WIDTH, channels), BF16),
            pltpu.VMEM((1, WIDTH), F32),
            pltpu.VMEM((SEQS * ROWS, 128), F32),
            pltpu.VMEM((SEQS * ROWS, 128), F32),
            pltpu.VMEM((2 * WIDTH, channels), F32),
            pltpu.VMEM((3, WIDTH, 128), F32),
            pltpu.VMEM((FLAT, 128), F32),
            pltpu.VMEM((FLAT, 128), F32),
            pltpu.SemaphoreType.DMA((SEQS // STEP,)),
            pltpu.SemaphoreType.DMA((7,)),
        ],
        compiler_params=pltpu.CompilerParams(vmem_limit_bytes=PROJECT_VMEM),
        cost_estimate=pl.CostEstimate(
            flops=2 * 6144 * 256 * 64, bytes_accessed=4 << 20, transcendentals=6144
        ),
        name="project",
    )(
        depth,
        lines,
        scale.reshape(1, -1),
        shift.reshape(1, -1),
        first.T,
        first_bias.reshape(1, -1),
        other.T,
        other_bias.reshape(1, -1),
    )


def tiles_kernel(distances, either, fresh, total, *refs):
    count = len(distances)
    me = lax.axis_index("res")
    side = 1 - 2 * (me % 2)
    depth_hbm, left_ref, *rest = refs
    given = count + int(either)
    right_refs, rest = rest[:given], rest[given:]
    final_in, bias_hbm, couple_hbm, *rest = rest
    if fresh:
        out_hbm, final_ref, *rest = rest
        *rest, final_raw, final_wide = rest
    else:
        final_ref = final_in
        _, out_hbm, *rest = rest
    (
        depth_ref,
        bias_ref,
        picked_ref,
        couple_buf,
        out_buf,
        small_sem,
        take_sem,
        give_sem,
    ) = rest
    blocks = [me + by(side) for by in distances]

    def columns(b):
        place = jnp.clip(blocks[b] - me + WIN, 0, 2 * WIN)
        return pl.ds(pl.multiple_of(place * ROWS, 8), ROWS)

    if fresh:
        final_take = pltpu.make_async_copy(final_in, final_raw, small_sem.at[2])
        final_take.start()
    small = start_all((depth_hbm, bias_hbm), (depth_ref, bias_ref), small_sem)
    takes = start_all(
        [couple_hbm.at[:, :, columns(b), :] for b in range(count)],
        [couple_buf.at[b] for b in range(count)],
        take_sem,
    )
    gives = [
        [
            pltpu.make_async_copy(
                out_buf.at[b, v], out_hbm.at[:, v, columns(b), :], give_sem.at[b, v]
            )
            for b in range(count)
        ]
        for v in range(4)
    ]
    if fresh:
        final_take.wait()
        final_wide[...] = final_raw[...].astype(F32)
        for y in range(0, WIDTH, 2):
            final_ref[y * WIDTH : (y + 2) * WIDTH, :] = jnp.concatenate(
                [final_wide[pl.ds(y + o, WIDTH, stride=WIDTH), :] for o in range(2)], axis=0
            ).astype(BF16)
    if either:
        picked_ref[...] = jnp.where(side > 0, right_refs[-2][...], right_refs[-1][...])
        right_refs = [*right_refs[:-2], picked_ref]

    group = lax.broadcasted_iota(jnp.int32, (count * 144, 128), 1) // WIDTH
    odd = (group & 1) == 1
    upper = (group & 2) == 2

    def turned(ref, parts, k):
        return jnp.concatenate(
            [
                ref[(4 * p + (g ^ k)) * WIDTH : (4 * p + (g ^ k) + 1) * WIDTH, :]
                for p in range(parts)
                for g in range(4)
            ],
            axis=0,
        )

    parts = []
    for k in range(4):
        outer = lax.dot_general(
            jnp.concatenate([right[k * 192 : (k + 1) * 192, :] for right in right_refs], axis=0),
            turned(left_ref, 6, k),
            NT,
            preferred_element_type=F32,
        )
        parts.append(
            [
                jnp.concatenate(
                    [
                        outer[
                            b * 192 + q * ROWS : b * 192 + (q + 1) * ROWS, h * 128 : (h + 1) * 128
                        ]
                        for b in range(count)
                        for h in range(6)
                    ],
                    axis=0,
                ).astype(BF16)
                for q in range(8)
            ]
        )
    mixed = [[], [], [], []]
    for q in range(8):
        pair = [jnp.where(odd, parts[k ^ 1][q], parts[k][q]) for k in range(4)]
        for v in range(4):
            mixed[v].append(jnp.where(upper, pair[v ^ 2], pair[v]))
    shares = []
    for b in range(count):
        depth_row = right_refs[b][FLAT : FLAT + 16, :128].astype(F32)[:1, :]
        depth_cols = jnp.broadcast_to(as_column(depth_row, ROWS), (ROWS, 128))
        inside = ((blocks[b] >= 0) & (blocks[b] < total)).astype(F32)
        shares.append((depth_cols, inside))
    for copy in small:
        copy.wait()
    bias = bias_ref[...]
    for v in range(4):
        sums = jnp.dot(
            jnp.concatenate(mixed[v], axis=1),
            turned(final_ref, 8, v),
            preferred_element_type=F32,
        )
        for b in range(count):
            if v == 0:
                takes[b].wait()
            depth_cols, inside = shares[b]
            for h in range(6):
                depth = depth_ref[4 * h + v].astype(F32)
                pairs = jnp.maximum(jnp.minimum(depth_cols, depth), 1.0)
                update = sums[(b * 6 + h) * ROWS : (b * 6 + h + 1) * ROWS] + bias
                out_buf[b, v, h] = couple_buf[b, h, v] + update * (inside / pairs)
            gives[v][b].start()
    for copies in gives:
        for copy in copies:
            copy.wait()


def form_tiles(distances, either, total, depth, left, rights, final, final_bias, couple, out, name):
    count = len(distances)
    fresh = out is None
    args = [depth, left, *rights, final, final_bias, couple]
    specs = [HBM, VMEM] + [VMEM] * len(rights) + [HBM if fresh else VMEM, HBM, HBM]
    alias = {}
    out_specs = [HBM]
    out_shape = [jax.ShapeDtypeStruct(couple.shape, couple.dtype)]
    extra = []
    if fresh:
        out_specs.append(VMEM)
        out_shape.append(jax.ShapeDtypeStruct(final.shape, final.dtype))
        extra = [pltpu.VMEM(final.shape, BF16), pltpu.VMEM(final.shape, F32)]
    else:
        alias = {len(args): 0}
        args.append(out)
        specs.append(HBM)
    return pl.pallas_call(
        functools.partial(tiles_kernel, distances, either, fresh, total),
        in_specs=specs,
        out_specs=out_specs,
        out_shape=out_shape,
        input_output_aliases=alias,
        scratch_shapes=[
            pltpu.SMEM((ROWS,), jnp.int32),
            pltpu.VMEM((1, 128), F32),
            pltpu.VMEM((SENT, SEQS), BF16),
            pltpu.VMEM((count, 6, 4, ROWS, 128), F32),
            pltpu.VMEM((count, 4, 6, ROWS, 128), F32),
            pltpu.SemaphoreType.DMA((3,)),
            pltpu.SemaphoreType.DMA((count,)),
            pltpu.SemaphoreType.DMA((count, 4)),
            *extra,
        ],
        compiler_params=pltpu.CompilerParams(vmem_limit_bytes=TILES_VMEM),
        cost_estimate=pl.CostEstimate(
            flops=count, bytes_accessed=count, transcendentals=0
        ),
        name=name,
    )(*args)


def on_device(
    homolog_features,
    standardize_scale,
    standardize_shift,
    first_map_matrix,
    first_map_intercept,
    other_map_matrix,
    other_map_intercept,
    final_map_matrix,
    final_map_intercept,
    coverage_lengths,
    couple_features,
):
    total = lax.axis_size("res")
    def passed(block):
        path = [*range(0, total, 2), *range(total - 1, 0, -2)]
        return lax.ppermute(block, "res", list(zip(path, path[1:] + path[:1])))

    def swapped(block):
        return lax.ppermute(block, "res", [(i, i ^ 1) for i in range(total)])

    left, own = project(
        homolog_features,
        coverage_lengths,
        standardize_scale,
        standardize_shift,
        first_map_matrix,
        first_map_intercept,
        other_map_matrix,
        other_map_intercept,
    )
    final_bias = final_map_intercept.reshape(1, -1)

    def tiles(distances, rights, final, out, name, either=False):
        return form_tiles(
            distances,
            either,
            total,
            coverage_lengths,
            left,
            rights,
            final,
            final_bias,
            couple,
            out,
            name,
        )

    couple = couple_features.reshape(ROWS // 4, 4, *couple_features.shape[1:])
    sibling = swapped(own)
    own_next = passed(own)
    sibling_next = passed(sibling)
    out, final = tiles(
        [lambda side: 0, lambda side: side],
        [own, sibling],
        final_map_matrix,
        None,
        "near",
    )
    own_next, sibling_next, out = lax.optimization_barrier((own_next, sibling_next, out))
    own_far = passed(own_next)
    sibling_far = passed(sibling_next)
    own_across = swapped(own_next)
    sibling_across = swapped(sibling_next)
    (out,) = tiles(
        [
            lambda side: -2 * side,
            lambda side: -side,
            lambda side: 3 * side,
            lambda side: 2 * side,
        ],
        [own_next, sibling_next, own_across, sibling_across],
        final,
        out,
        "middle",
    )
    own_far, sibling_far, out = lax.optimization_barrier((own_far, sibling_far, out))
    last = swapped(sibling_far)
    (out,) = tiles(
        [lambda side: -4 * side, lambda side: -3 * side], [own_far, sibling_far], final, out, "far"
    )
    (out,) = tiles([lambda side: 4 * side], [last], final, out, "last")
    return out.reshape(couple_features.shape)


def solution(mesh):
    return jax.shard_map(
        on_device,
        mesh=mesh,
        in_specs=(
            P(None, "res", None),
            P(),
            P(),
            P(),
            P(),
            P(),
            P(),
            P(),
            P(),
            P("res"),
            P("res", None, None),
        ),
        out_specs=P("res", None, None),
        check_vma=False,
    )
```

```python
import functools

import jax
import jax.numpy as jnp
from jax import lax
from jax.experimental import pallas as pl
from jax.experimental.pallas import tpu as pltpu
from jax.sharding import PartitionSpec as P

WIN = 4
ROWS = 24
WIDTH = 32
SEQS = 256
STEP = 64
PART = 32
FLAT = ROWS * WIDTH
SENT = FLAT + 16

PROJECT_VMEM = 60 << 20
TILES_VMEM = 44 << 20

BF16 = jnp.bfloat16
F32 = jnp.float32
NT = (((1,), (1,)), ((), ()))


def as_column(row, count):
    width = row.shape[1]
    wide = jnp.broadcast_to(row, (count, width))
    at = lax.broadcasted_iota(jnp.int32, (count, width), 1)
    down = lax.broadcasted_iota(jnp.int32, (count, width), 0)
    return jnp.sum(jnp.where(at == down, wide, 0.0), axis=1, keepdims=True)


HBM = pl.BlockSpec(memory_space=pltpu.HBM)
VMEM = pl.BlockSpec(memory_space=pltpu.VMEM)


def start_all(sources, targets, sems):
    copies = [
        pltpu.make_async_copy(source, target, sems.at[n])
        for n, (source, target) in enumerate(zip(sources, targets))
    ]
    for copy in copies:
        copy.start()
    return copies


def project_kernel(
    depth_hbm,
    lines_hbm,
    scale_hbm,
    shift_hbm,
    first_hbm,
    first_bias_hbm,
    other_hbm,
    other_bias_hbm,
    left_ref,
    right_ref,
    depth_ref,
    lines_ref,
    scale_ref,
    shift_ref,
    first_ref,
    first_bias_ref,
    other_ref,
    other_bias_ref,
    low_ref,
    high_ref,
    maps_ref,
    turn_ref,
    right_low_ref,
    right_high_ref,
    lines_sem,
    small_sem,
):
    steps = SEQS // STEP

    def fetch(s):
        at = pl.ds(pl.multiple_of(s * STEP, STEP), STEP)
        return pltpu.make_async_copy(lines_hbm.at[at], lines_ref.at[at], lines_sem.at[s])

    fetch(0).start()
    small = start_all(
        (scale_hbm, shift_hbm, first_hbm, first_bias_hbm, other_hbm, other_bias_hbm, depth_hbm),
        (scale_ref, shift_ref, first_ref, first_bias_ref, other_ref, other_bias_ref, depth_ref),
        small_sem,
    )
    for s in range(1, steps):
        fetch(s).start()
    for copy in small:
        copy.wait()

    maps_ref[:WIDTH, :] = first_ref[...].astype(F32)
    turned = other_ref[...].astype(F32)
    first_bias = as_column(first_bias_ref[...], WIDTH)
    other_bias = jnp.broadcast_to(as_column(other_bias_ref[...], WIDTH), (WIDTH, 128))
    turn_ref[0] = turned[:, :128]
    turn_ref[1] = turned[:, 128:]
    turn_ref[2] = other_bias
    biases = [jnp.broadcast_to(first_bias, (WIDTH, 128))]
    for k in range(4):
        for half in range(2):
            maps_ref[WIDTH + 8 * k : WIDTH + 8 * k + 8, half * 128 : half * 128 + 128] = turn_ref[
                half, pl.ds(k, 8, stride=4), :
            ]
        biases.append(turn_ref[2, pl.ds(k, 8, stride=4), :])
    bias = jnp.concatenate(biases, axis=0)
    bias = jnp.concatenate([bias, bias], axis=1)
    maps = maps_ref[...].astype(BF16)
    scale = scale_ref[...]
    shift = shift_ref[...]

    def normalise(s, carry):
        fetch(s).wait()
        for c in range(STEP // PART):
            at = pl.ds(pl.multiple_of(s * STEP + c * PART, PART), PART)
            x = lines_ref[at].astype(F32).reshape(PART * ROWS, -1)
            centred = x - jnp.mean(x, axis=1, keepdims=True)
            variance = jnp.mean(centred * centred, axis=1, keepdims=True)
            normed = centred * lax.rsqrt(variance + 1e-05) * scale + shift
            at = pl.ds(pl.multiple_of((s * STEP + c * PART) * ROWS, 8), PART * ROWS)
            low_ref[at, :] = normed[:, :128]
            high_ref[at, :] = normed[:, 128:]
        return carry

    lax.fori_loop(0, steps, normalise, 0)

    seq = lax.broadcasted_iota(jnp.int32, (2 * WIDTH, SEQS), 1)
    lane = lax.broadcasted_iota(jnp.int32, (16, SEQS), 1)
    depths = jnp.zeros((16, SEQS), F32)
    for i in range(ROWS):
        depth = depth_ref[i]
        rows = jnp.concatenate(
            [low_ref[pl.ds(i, SEQS, stride=ROWS), :], high_ref[pl.ds(i, SEQS, stride=ROWS), :]],
            axis=1,
        ).astype(BF16)
        both = lax.dot_general(maps, rows, NT, preferred_element_type=F32) + bias
        both = jnp.where(seq < depth, both, 0.0)
        left_ref[i * WIDTH : (i + 1) * WIDTH, :] = both[:WIDTH].astype(BF16)
        right_low_ref[pl.ds(i, WIDTH, stride=ROWS), :] = both[WIDTH:, :128]
        right_high_ref[pl.ds(i, WIDTH, stride=ROWS), :] = both[WIDTH:, 128:]
        depths = jnp.where(lane == i, depth.astype(F32), depths)
    right_ref[:FLAT, :128] = right_low_ref[...].astype(BF16)
    right_ref[:FLAT, 128:] = right_high_ref[...].astype(BF16)
    right_ref[FLAT:, :] = depths.astype(BF16)


def project(lines, depth, scale, shift, first, first_bias, other, other_bias):
    channels = lines.shape[2]
    return pl.pallas_call(
        project_kernel,
        in_specs=[HBM] * 8,
        out_specs=[VMEM] * 2,
        out_shape=[
            jax.ShapeDtypeStruct((FLAT, SEQS), BF16),
            jax.ShapeDtypeStruct((SENT, SEQS), BF16),
        ],
        scratch_shapes=[
            pltpu.SMEM((ROWS,), jnp.int32),
            pltpu.VMEM((SEQS, ROWS, channels), BF16),
            pltpu.VMEM((1, channels), F32),
            pltpu.VMEM((1, channels), F32),
            pltpu.VMEM((WIDTH, channels), BF16),
            pltpu.VMEM((1, WIDTH), F32),
            pltpu.VMEM((WIDTH, channels), BF16),
            pltpu.VMEM((1, WIDTH), F32),
            pltpu.VMEM((SEQS * ROWS, 128), F32),
            pltpu.VMEM((SEQS * ROWS, 128), F32),
            pltpu.VMEM((2 * WIDTH, channels), F32),
            pltpu.VMEM((3, WIDTH, 128), F32),
            pltpu.VMEM((FLAT, 128), F32),
            pltpu.VMEM((FLAT, 128), F32),
            pltpu.SemaphoreType.DMA((SEQS // STEP,)),
            pltpu.SemaphoreType.DMA((7,)),
        ],
        compiler_params=pltpu.CompilerParams(vmem_limit_bytes=PROJECT_VMEM),
        cost_estimate=pl.CostEstimate(
            flops=2 * 6144 * 256 * 64, bytes_accessed=4 << 20, transcendentals=6144
        ),
        name="project",
    )(
        depth,
        lines,
        scale.reshape(1, -1),
        shift.reshape(1, -1),
        first.T,
        first_bias.reshape(1, -1),
        other.T,
        other_bias.reshape(1, -1),
    )


def tiles_kernel(distances, either, fresh, total, *refs):
    count = len(distances)
    me = lax.axis_index("res")
    side = 1 - 2 * (me % 2)
    depth_hbm, left_ref, *rest = refs
    given = count + int(either)
    right_refs, rest = rest[:given], rest[given:]
    final_in, bias_hbm, couple_hbm, *rest = rest
    if fresh:
        out_hbm, final_ref, *rest = rest
        *rest, final_raw, final_wide = rest
    else:
        final_ref = final_in
        _, out_hbm, *rest = rest
    (
        depth_ref,
        bias_ref,
        picked_ref,
        couple_buf,
        out_buf,
        small_sem,
        take_sem,
        give_sem,
    ) = rest
    blocks = [me + by(side) for by in distances]

    def columns(b):
        place = jnp.clip(blocks[b] - me + WIN, 0, 2 * WIN)
        return pl.ds(pl.multiple_of(place * ROWS, 8), ROWS)

    if fresh:
        final_take = pltpu.make_async_copy(final_in, final_raw, small_sem.at[2])
        final_take.start()
    small = start_all((depth_hbm, bias_hbm), (depth_ref, bias_ref), small_sem)
    takes = start_all(
        [couple_hbm.at[:, :, columns(b), :] for b in range(count)],
        [couple_buf.at[b] for b in range(count)],
        take_sem,
    )
    gives = [
        [
            pltpu.make_async_copy(
                out_buf.at[b, v], out_hbm.at[:, v, columns(b), :], give_sem.at[b, v]
            )
            for b in range(count)
        ]
        for v in range(4)
    ]
    if fresh:
        final_take.wait()
        final_wide[...] = final_raw[...].astype(F32)
        for y in range(0, WIDTH, 2):
            final_ref[y * WIDTH : (y + 2) * WIDTH, :] = jnp.concatenate(
                [final_wide[pl.ds(y + o, WIDTH, stride=WIDTH), :] for o in range(2)], axis=0
            ).astype(BF16)
    if either:
        picked_ref[...] = jnp.where(side > 0, right_refs[-2][...], right_refs[-1][...])
        right_refs = [*right_refs[:-2], picked_ref]

    group = lax.broadcasted_iota(jnp.int32, (count * 144, 128), 1) // WIDTH
    odd = (group & 1) == 1
    upper = (group & 2) == 2

    def turned(ref, parts, k):
        return jnp.concatenate(
            [
                ref[(4 * p + (g ^ k)) * WIDTH : (4 * p + (g ^ k) + 1) * WIDTH, :]
                for p in range(parts)
                for g in range(4)
            ],
            axis=0,
        )

    parts = []
    for k in range(4):
        outer = lax.dot_general(
            jnp.concatenate([right[k * 192 : (k + 1) * 192, :] for right in right_refs], axis=0),
            turned(left_ref, 6, k),
            NT,
            preferred_element_type=F32,
        )
        parts.append(
            [
                jnp.concatenate(
                    [
                        outer[
                            b * 192 + q * ROWS : b * 192 + (q + 1) * ROWS, h * 128 : (h + 1) * 128
                        ]
                        for b in range(count)
                        for h in range(6)
                    ],
                    axis=0,
                ).astype(BF16)
                for q in range(8)
            ]
        )
    mixed = [[], [], [], []]
    for q in range(8):
        pair = [jnp.where(odd, parts[k ^ 1][q], parts[k][q]) for k in range(4)]
        for v in range(4):
            mixed[v].append(jnp.where(upper, pair[v ^ 2], pair[v]))
    shares = []
    for b in range(count):
        depth_row = right_refs[b][FLAT : FLAT + 16, :128].astype(F32)[:1, :]
        depth_cols = jnp.broadcast_to(as_column(depth_row, ROWS), (ROWS, 128))
        inside = ((blocks[b] >= 0) & (blocks[b] < total)).astype(F32)
        shares.append((depth_cols, inside))
    for copy in small:
        copy.wait()
    bias = bias_ref[...]
    for v in range(4):
        sums = jnp.dot(
            jnp.concatenate(mixed[v], axis=1),
            turned(final_ref, 8, v),
            preferred_element_type=F32,
        )
        for b in range(count):
            if v == 0:
                takes[b].wait()
            depth_cols, inside = shares[b]
            for h in range(6):
                depth = depth_ref[4 * h + v].astype(F32)
                pairs = jnp.maximum(jnp.minimum(depth_cols, depth), 1.0)
                update = sums[(b * 6 + h) * ROWS : (b * 6 + h + 1) * ROWS] + bias
                out_buf[b, v, h] = couple_buf[b, h, v] + update * (inside / pairs)
            gives[v][b].start()
    for copies in gives:
        for copy in copies:
            copy.wait()


def form_tiles(distances, either, total, depth, left, rights, final, final_bias, couple, out, name):
    count = len(distances)
    fresh = out is None
    args = [depth, left, *rights, final, final_bias, couple]
    specs = [HBM, VMEM] + [VMEM] * len(rights) + [HBM if fresh else VMEM, HBM, HBM]
    alias = {}
    out_specs = [HBM]
    out_shape = [jax.ShapeDtypeStruct(couple.shape, couple.dtype)]
    extra = []
    if fresh:
        out_specs.append(VMEM)
        out_shape.append(jax.ShapeDtypeStruct(final.shape, final.dtype))
        extra = [pltpu.VMEM(final.shape, BF16), pltpu.VMEM(final.shape, F32)]
    else:
        alias = {len(args): 0}
        args.append(out)
        specs.append(HBM)
    return pl.pallas_call(
        functools.partial(tiles_kernel, distances, either, fresh, total),
        in_specs=specs,
        out_specs=out_specs,
        out_shape=out_shape,
        input_output_aliases=alias,
        scratch_shapes=[
            pltpu.SMEM((ROWS,), jnp.int32),
            pltpu.VMEM((1, 128), F32),
            pltpu.VMEM((SENT, SEQS), BF16),
            pltpu.VMEM((count, 6, 4, ROWS, 128), F32),
            pltpu.VMEM((count, 4, 6, ROWS, 128), F32),
            pltpu.SemaphoreType.DMA((3,)),
            pltpu.SemaphoreType.DMA((count,)),
            pltpu.SemaphoreType.DMA((count, 4)),
            *extra,
        ],
        compiler_params=pltpu.CompilerParams(vmem_limit_bytes=TILES_VMEM),
        cost_estimate=pl.CostEstimate(
            flops=count, bytes_accessed=count, transcendentals=0
        ),
        name=name,
    )(*args)


def on_device(
    homolog_features,
    standardize_scale,
    standardize_shift,
    first_map_matrix,
    first_map_intercept,
    other_map_matrix,
    other_map_intercept,
    final_map_matrix,
    final_map_intercept,
    coverage_lengths,
    couple_features,
):
    total = lax.axis_size("res")
    def passed(block):
        path = [*range(0, total, 2), *range(total - 1, 0, -2)]
        return lax.ppermute(block, "res", list(zip(path, path[1:] + path[:1])))

    def swapped(block):
        return lax.ppermute(block, "res", [(i, i ^ 1) for i in range(total)])

    left, own = project(
        homolog_features,
        coverage_lengths,
        standardize_scale,
        standardize_shift,
        first_map_matrix,
        first_map_intercept,
        other_map_matrix,
        other_map_intercept,
    )
    final_bias = final_map_intercept.reshape(1, -1)

    def tiles(distances, rights, final, out, name, either=False):
        return form_tiles(
            distances,
            either,
            total,
            coverage_lengths,
            left,
            rights,
            final,
            final_bias,
            couple,
            out,
            name,
        )

    couple = couple_features.reshape(ROWS // 4, 4, *couple_features.shape[1:])
    sibling = swapped(own)
    own_next = passed(own)
    sibling_next = passed(sibling)
    out, final = tiles(
        [lambda side: 0, lambda side: side],
        [own, sibling],
        final_map_matrix,
        None,
        "near",
    )
    own_next, sibling_next, out = lax.optimization_barrier((own_next, sibling_next, out))
    sibling_far = passed(sibling_next)
    own_far = passed(own_next)
    own_across = swapped(own_next)
    sibling_across = swapped(sibling_next)
    (out,) = tiles(
        [
            lambda side: -2 * side,
            lambda side: -side,
            lambda side: 3 * side,
            lambda side: 2 * side,
        ],
        [own_next, sibling_next, own_across, sibling_across],
        final,
        out,
        "middle",
    )
    sibling_far, out = lax.optimization_barrier((sibling_far, out))
    last = swapped(sibling_far)
    (out,) = tiles(
        [lambda side: -4 * side, lambda side: -3 * side, lambda side: 4 * side],
        [own_far, sibling_far, last],
        final,
        out,
        "far",
    )
    return out.reshape(couple_features.shape)


def solution(mesh):
    return jax.shard_map(
        on_device,
        mesh=mesh,
        in_specs=(
            P(None, "res", None),
            P(),
            P(),
            P(),
            P(),
            P(),
            P(),
            P(),
            P(),
            P("res"),
            P("res", None, None),
        ),
        out_specs=P("res", None, None),
        check_vma=False,
    )
```
